512 devices in a mesh: dp: 64 (over x, z), tensor: 8 (over y, core).
Axes of the slice: x: 4, y: 4, z: 16, core: 2. Of those that a mesh axis runs over, the one named last changes fastest.
Arguments:
- grad: bfloat16 [64, 768, 8192], P('dp', None, 'tensor'), may hold values from -6 to 6
- residual: bfloat16 [64, 768, 8192], P('dp', None, 'tensor'), may hold values from -4 to 4
- counts: int32 [64], P('dp'), may hold values from 1000 to 3499
- q_start: float32 [64, 8192], P(None, 'tensor'), may hold values from -0.0625 to 0.0625
Outputs:
- new_residual: bfloat16 [64, 768, 8192], P('dp', None, 'tensor')
- q_final: float32 [64, 8192], P(None, 'tensor')
The draws below stay inside these ranges and needn't reach their ends.
All inputs are finite; a program needn't handle non-finite values.
Results may differ from the reference program's by a relative error of at most 0.001.
Values sent between devices are 32-bit elements; how exact they have to be, the bound alone decides.
A program may use at most 64 MiB of HBM per device.

```python
import jax
import jax.numpy as jnp
from jax import lax

ROWS = 768
RANK = 64
ITERS = 2
COLS = 8192
REPLICAS = 64


def draw_counts(key, part):
    key = jax.random.fold_in(key, 7)
    position = jnp.arange(REPLICAS, dtype=jnp.int32)
    base = 1000 + 2000 * position // max(REPLICAS - 1, 1)
    jitter = jax.random.randint(key, (REPLICAS,), 0, 500, dtype=jnp.int32)
    return (base + jitter).astype(jnp.int32)


def steps_of(rng, shape, pieces, least, largest):
    def one(dim, blocks):
        draws = jax.random.uniform(jax.random.fold_in(jax.random.fold_in(rng, 6), dim), (blocks,), jnp.float32, least / len(pieces), largest / len(pieces))
        return jnp.repeat(jnp.exp(draws), shape[dim] // blocks).reshape((-1,) + (1,) * (len(shape) - dim - 1))

    level = one(*pieces[0])
    for cut in pieces[1:]:
        level = level * one(*cut)
    return level


def gaussian(stream_key, dims, width, bound, pieces=(), held_as=jnp.bfloat16):
    result = jax.random.normal(stream_key, dims, jnp.float32) * width
    if len(pieces) > 0:
        result = steps_of(stream_key, dims, pieces, -0.22, 0.18) * result
    return jnp.clip(result, min=-bound, max=bound).astype(held_as)


def setup_inputs(seed: int = 0) -> dict:
    splits = jax.random.split(jax.random.key(seed), 5)
    grad = gaussian(splits[0], (REPLICAS, ROWS, COLS), 1.0, 6.0, ((0, 64), (2, 8)))
    residual = gaussian(splits[1], (REPLICAS, ROWS, COLS), 0.5, 4.0, ((0, 64), (2, 8)))
    counts = draw_counts(jax.random.fold_in(splits[4], 71), 0)
    q_start = gaussian(splits[3], (RANK, COLS), COLS ** -0.5, 0.0625, ((1, 8),), jnp.float32)
    return dict(grad=grad, residual=residual, counts=counts, q_start=q_start)


def reference(grad, residual, counts, q_start):
    highest = lax.Precision.HIGHEST
    count_float = counts.astype(jnp.float32)
    token_total = jnp.sum(count_float)
    weights = REPLICAS * count_float / token_total
    indices = jnp.arange(REPLICAS, dtype=jnp.int32)

    def matrix_of(index):
        gradient = lax.dynamic_index_in_dim(grad, index, 0, keepdims=False).astype(jnp.float32)
        carried = lax.dynamic_index_in_dim(residual, index, 0, keepdims=False).astype(jnp.float32)
        scale = lax.dynamic_index_in_dim(weights, index, 0, keepdims=False)
        return scale * gradient + carried
    q_basis = q_start
    p_basis = jnp.zeros((RANK, ROWS), jnp.float32)
    for step_index in range(ITERS):

        def left_step(accum, index):
            return (accum + jnp.einsum('kc,rc->kr', q_basis, matrix_of(index), precision=highest), None)
        p_sum, unused = lax.scan(left_step, jnp.zeros((RANK, ROWS), jnp.float32), indices)
        p_sum = p_sum / REPLICAS
        gram_matrix = jnp.dot(p_sum, p_sum.T, precision=highest)
        lower_factor = jnp.linalg.cholesky(gram_matrix)
        p_basis = jax.scipy.linalg.solve_triangular(lower_factor, p_sum, lower=True)

        def right_step(accum, index):
            return (accum + jnp.einsum('kr,rc->kc', p_basis, matrix_of(index), precision=highest), None)
        q_sum, unused = lax.scan(right_step, jnp.zeros((RANK, COLS), jnp.float32), indices)
        q_basis = q_sum / REPLICAS
    approx = jnp.einsum('kr,kc->rc', p_basis, q_basis, precision=highest)
    new_residual = lax.map(lambda index: (matrix_of(index) - approx).astype(jnp.bfloat16), indices)
    return (new_residual, q_basis)
```

```python
import jax
import jax.numpy as jnp
from jax import lax
from jax.sharding import PartitionSpec as P
import jax.experimental.pallas as pl
import jax.experimental.pallas.tpu as pltpu

MESH = pl.DeviceIdType.MESH
HIGHEST = lax.Precision.HIGHEST
F32 = jnp.float32
BF16 = jnp.bfloat16
ROWS, RANK, WIDTH, REPLICAS = 768, 64, 1024, 64
HALF = ROWS // 2
NX, NY, NZ = 4, 4, 16
NN = (((1,), (0,)), ((), ()))
NT = (((1,), (1,)), ((), ()))
PARTNERS = 43


def split(value):
    high = value.astype(BF16)
    low = (value - high.astype(F32)).astype(BF16)
    return jnp.concatenate([high, low], axis=0)


def fold(value):
    return value[:RANK] + value[RANK:]


def place(x, z, y, c):
    return (x * NZ + z, y * 2 + c)


def near_z(o):
    return jnp.where(o == 3, NZ - 1, o)


def kernel(counts, q_start, grad, residual, new_residual, q_final,
           g, r, out, load_sem, store_sem,
           count_x, count_z, count_sem,
           part1, core1, rows1, zs1, part2, core2, rows2, zs2, pf, p_sem,
           qs, near, far, qf, q_sem, elim, p_left):
    dp = lax.axis_index("dp")
    tensor = lax.axis_index("tensor")
    x, z, y, c = dp // NZ, dp % NZ, tensor // 2, tensor % 2
    me = x * NY + y

    load_g = pltpu.make_async_copy(grad.at[0], g, load_sem.at[0])
    load_r = pltpu.make_async_copy(residual.at[0], r, load_sem.at[1])
    load_g.start()
    load_r.start()

    def core_peer():
        return place(x, z, y, 1 - c)

    def xy_peer(j):
        return (x + j % 4) % 4, (y + j // 4) % 4

    barrier = pltpu.get_barrier_semaphore()

    def announce(device):
        pl.semaphore_signal(barrier, inc=1, device_id=device, device_id_type=MESH)

    def announce_z(k, carry):
        announce(place(x, (z + k) % NZ, y, c))
        return carry

    def announce_xy(j, carry):
        px, py = xy_peer(j)
        announce(place(px, z, py, c))
        return carry

    def announce_xz(i, carry):
        o = i // 3
        dz = jnp.where(o < 2, o + 1, o + 12)
        announce(place((x + i % 3 + 1) % 4, (z + dz) % NZ, y, c))
        return carry

    lax.fori_loop(1, 16, announce_z, 0)
    lax.fori_loop(1, 16, announce_xy, 0)
    lax.fori_loop(0, 12, announce_xz, 0)
    announce(core_peer())

    def send(src, dst, sems, device):
        pltpu.make_async_remote_copy(
            src_ref=src, dst_ref=dst, send_sem=sems.at[0], recv_sem=sems.at[1],
            device_id=device, device_id_type=MESH,
        ).start()

    def took(ref, sem):
        pltpu.make_async_copy(ref, ref, sem).wait()

    def left_sum(step, part, core, rows, zs, finish, beside):
        sems = p_sem.at[step]
        send(part.at[1 - c], core, sems.at[0], core_peer())
        took(core, sems.at[0, 1])
        part[c] = part[c] + core[...]

        def to_xy(j, carry):
            px, py = xy_peer(j)
            send(part.at[c, px * NY + py], rows.at[j - 1], sems.at[1], place(px, z, py, c))
            return carry

        lax.fori_loop(1, 16, to_xy, 0)
        beside()
        took(rows, sems.at[1, 1])
        zs[z] = part[c, me] + jnp.sum(rows[...], axis=0)

        def to_z(k, carry):
            send(zs.at[z], zs.at[z], sems.at[2], place(x, (z + k) % NZ, y, c))
            return carry

        lax.fori_loop(1, 16, to_z, 0)
        took(zs.at[pl.ds(0, 15)], sems.at[2, 1])
        pf[step, c, me] = finish(jnp.sum(zs[...], axis=0))

        def spread(j, carry):
            px, py = xy_peer(j)
            send(pf.at[step, c, me], pf.at[step, c, me], sems.at[3], place(px, z, py, c))
            return carry

        lax.fori_loop(1, 16, spread, 0)
        took(pf.at[step, c, pl.ds(0, 15)], sems.at[3, 1])
        send(pf.at[step, c], pf.at[step, c], sems.at[4], core_peer())
        took(pf.at[step, 1 - c], sems.at[4, 1])
        took(core, sems.at[0, 0])
        took(rows, sems.at[1, 0])
        took(zs.at[pl.ds(0, 15)], sems.at[2, 0])
        took(pf.at[step, c, pl.ds(0, 15)], sems.at[3, 0])
        took(pf.at[step, c], sems.at[4, 0])
        halves = [
            jnp.concatenate([pf[step, h, s] for s in range(16)], axis=0) for h in range(2)
        ]
        return jnp.concatenate(halves, axis=1)

    def eliminate(first, last):
        lane = lax.broadcasted_iota(jnp.int32, (RANK, 2 * RANK), 1)
        sub = lax.broadcasted_iota(jnp.int32, (RANK, 1), 0)

        def one(j, carry):
            rows = elim[...]
            pivot = elim[pl.ds(j, 1), :]
            here = lane == (j + RANK)
            column = jnp.sum(jnp.where(here, rows, 0.0), axis=1, keepdims=True)
            diagonal = jnp.sum(jnp.where(here[:1], pivot, 0.0), axis=1, keepdims=True)
            factor = jnp.where(sub > j, column / diagonal, 0.0)
            elim[...] = rows - factor * pivot
            return carry

        lax.fori_loop(first, last, one, 0)

    def inverse():
        lane = lax.broadcasted_iota(jnp.int32, (RANK, 2 * RANK), 1)
        sub = lax.broadcasted_iota(jnp.int32, (RANK, 2 * RANK), 0)
        rows = elim[...]
        diagonal = jnp.sum(jnp.where(lane == sub + RANK, rows, 0.0), axis=1, keepdims=True)
        return rows[:, :RANK] / jnp.sqrt(diagonal)

    def right_sum(step, p_sum, weight):
        sems = q_sem.at[step]
        plain, weighted = split(p_sum), split(weight * p_sum)
        for jx in range(NX):
            cols = slice(256 * jx, 256 * (jx + 1))
            terms = fold(
                lax.dot_general(weighted, g[:, cols], NN, preferred_element_type=F32)
                + lax.dot_general(plain, r[:, cols], NN, preferred_element_type=F32)
            )
            for jz in range(4):
                qs[step, 4 * jx + jz] = terms[16 * jz:16 * (jz + 1)]
        slot = x * 4 + z % 4

        def to_near(i, carry):
            px, pz = (x + i % 4) % 4, (z + near_z(i // 4)) % NZ
            send(qs.at[step, px * 4 + pz % 4], near.at[step, i - 1], sems.at[0], place(px, pz, y, c))
            return carry

        lax.fori_loop(1, 16, to_near, 0)
        elim[...] = lax.dot_general(
            p_sum, jnp.concatenate([jnp.zeros_like(p_sum), p_sum], axis=0), NT,
            precision=HIGHEST, preferred_element_type=F32,
        ) + jnp.where(
            lax.broadcasted_iota(jnp.int32, (RANK, 2 * RANK), 0)
            == lax.broadcasted_iota(jnp.int32, (RANK, 2 * RANK), 1), 1.0, 0.0,
        )
        eliminate(0, 32)
        took(near.at[step], sems.at[0, 1])
        block = z // 4
        far[step, block] = qs[step, slot] + jnp.sum(near[step], axis=0)

        def to_far(k, carry):
            send(far.at[step, block], far.at[step, block], sems.at[1], place(x, (z + 4 * k) % NZ, y, c))
            return carry

        lax.fori_loop(1, 4, to_far, 0)
        eliminate(32, 64)
        lower_inverse = inverse()
        took(far.at[step, pl.ds(0, 3)], sems.at[1, 1])
        qf[step, slot] = jnp.sum(far[step], axis=0)

        def spread(i, carry):
            px, pz = (x + i % 4) % 4, (z + NZ - near_z(i // 4)) % NZ
            send(qf.at[step, slot], qf.at[step, slot], sems.at[2], place(px, pz, y, c))
            return carry

        lax.fori_loop(1, 16, spread, 0)
        p_basis = lax.dot_general(lower_inverse, p_sum, NN, precision=HIGHEST, preferred_element_type=F32)
        took(qf.at[step, pl.ds(0, 15)], sems.at[2, 1])
        took(near.at[step], sems.at[0, 0])
        took(far.at[step, pl.ds(0, 3)], sems.at[1, 0])
        took(qf.at[step, pl.ds(0, 15)], sems.at[2, 0])
        q_sum = jnp.concatenate(
            [jnp.concatenate([qf[step, 4 * jx + jz] for jz in range(4)], axis=0) for jx in range(NX)], axis=1
        )
        q_basis = lax.dot_general(
            lower_inverse, q_sum * (1.0 / REPLICAS), NN, precision=HIGHEST, preferred_element_type=F32
        )
        return p_basis, q_basis

    def put_part(ref, value, offset):
        for h in range(2):
            for s in range(16):
                ref[h, s, offset:offset + 4, :] = value[4 * s:4 * s + 4, HALF * h:HALF * (h + 1)]

    tokens = counts[0].astype(F32)
    first = split(q_start[...])
    load_g.wait()
    for n in range(3):
        rows = slice(256 * n, 256 * (n + 1))
        p_left[:, rows] = fold(lax.dot_general(first, g[rows], NT, preferred_element_type=F32)) * tokens
    put_part(part1, p_left[...], 0)
    load_r.wait()
    for n in range(3):
        rows = slice(256 * n, 256 * (n + 1))
        p_left[:, rows] = fold(lax.dot_general(first, r[rows], NT, preferred_element_type=F32))
    put_part(part1, p_left[...], 4)
    count_x[0] = jnp.full((8, 128), tokens, F32)
    pl.semaphore_wait(barrier, PARTNERS)

    def count_to_x(k, carry):
        send(count_x.at[0], count_x.at[k], count_sem.at[0], place((x + k) % 4, z, y, c))
        return carry

    lax.fori_loop(1, 4, count_to_x, 0)

    def count_over_z():
        took(count_x.at[pl.ds(1, 3)], count_sem.at[0, 1])
        count_z[z] = jnp.sum(count_x[...], axis=0)

        def count_to_z(k, carry):
            send(count_z.at[z], count_z.at[z], count_sem.at[1], place(x, (z + k) % NZ, y, c))
            return carry

        lax.fori_loop(1, 16, count_to_z, 0)

    def finish_first(total):
        took(count_z.at[pl.ds(0, 15)], count_sem.at[1, 1])
        all_tokens = jnp.sum(count_z[...], axis=0)[:1, :1]
        return (total[:4] * (REPLICAS / all_tokens) + total[4:]) * (1.0 / REPLICAS)

    p_sum = left_sum(0, part1, core1, rows1, zs1, finish_first, count_over_z)
    took(count_x.at[pl.ds(1, 3)], count_sem.at[0, 0])
    took(count_z.at[pl.ds(0, 15)], count_sem.at[1, 0])
    weight = REPLICAS * tokens / jnp.sum(count_z[...], axis=0)[:1, :1]
    p_basis, q_basis = right_sum(0, p_sum, weight)

    plain, weighted = split(q_basis), split(weight * q_basis)
    for n in range(3):
        rows = slice(256 * n, 256 * (n + 1))
        p_left[:, rows] = fold(
            lax.dot_general(weighted, g[rows], NT, preferred_element_type=F32)
            + lax.dot_general(plain, r[rows], NT, preferred_element_type=F32)
        )
    put_part(part2, p_left[...], 0)
    p_sum = left_sum(1, part2, core2, rows2, zs2, lambda total: total * (1.0 / REPLICAS), lambda: None)
    p_basis, q_basis = right_sum(1, p_sum, weight)

    q_final[...] = q_basis
    p_high = p_basis.astype(BF16).astype(F32)
    stacked = jnp.concatenate([p_high, p_basis - p_high, p_high], axis=0)
    left = stacked.T.astype(BF16)
    q_high = q_basis.astype(BF16)
    q_low = (q_basis - q_high.astype(F32)).astype(BF16)
    right = jnp.concatenate([q_high, q_high, q_low], axis=0)
    stores = []
    for n in range(6):
        rows = slice(128 * n, 128 * (n + 1))
        approx = lax.dot_general(left[rows], right, NN, preferred_element_type=F32)
        matrix = weight * g[rows].astype(F32) + r[rows].astype(F32)
        out[rows] = (matrix - approx).astype(BF16)
        store = pltpu.make_async_copy(out.at[rows], new_residual.at[0, rows], store_sem.at[n])
        store.start()
        stores.append(store)
    for store in stores:
        store.wait()


def local(grad, residual, counts, q_start):
    vmem = pl.BlockSpec(memory_space=pltpu.VMEM)
    anywhere = pl.BlockSpec(memory_space=pl.ANY)
    dma = pltpu.SemaphoreType.DMA
    return pl.pallas_call(
        kernel,
        out_shape=(
            jax.ShapeDtypeStruct((1, ROWS, WIDTH), BF16),
            jax.ShapeDtypeStruct((RANK, WIDTH), F32),
        ),
        in_specs=[pl.BlockSpec(memory_space=pltpu.SMEM), vmem, anywhere, anywhere],
        out_specs=(anywhere, vmem),
        scratch_shapes=[
            pltpu.VMEM((ROWS, WIDTH), BF16),
            pltpu.VMEM((ROWS, WIDTH), BF16),
            pltpu.VMEM((ROWS, WIDTH), BF16),
            dma((2,)),
            dma((6,)),
            pltpu.VMEM((4, 8, 128), F32),
            pltpu.VMEM((16, 8, 128), F32),
            dma((2, 2)),
            pltpu.VMEM((2, 16, 8, HALF), F32),
            pltpu.VMEM((16, 8, HALF), F32),
            pltpu.VMEM((15, 8, HALF), F32),
            pltpu.VMEM((16, 8, HALF), F32),
            pltpu.VMEM((2, 16, 4, HALF), F32),
            pltpu.VMEM((16, 4, HALF), F32),
            pltpu.VMEM((15, 4, HALF), F32),
            pltpu.VMEM((16, 4, HALF), F32),
            pltpu.VMEM((2, 2, 16, 4, HALF), F32),
            dma((2, 5, 2)),
            pltpu.VMEM((2, 16, 16, 256), F32),
            pltpu.VMEM((2, 15, 16, 256), F32),
            pltpu.VMEM((2, 4, 16, 256), F32),
            pltpu.VMEM((2, 16, 16, 256), F32),
            dma((2, 3, 2)),
            pltpu.VMEM((RANK, 2 * RANK), F32),
            pltpu.VMEM((RANK, ROWS), F32),
        ],
        compiler_params=pltpu.CompilerParams(
            collective_id=0, has_side_effects=True, vmem_limit_bytes=40 * 1024 * 1024
        ),
        name="power_step",
    )(counts, q_start, grad, residual)


def solution(mesh):
    placed = (P("dp", None, "tensor"), P("dp", None, "tensor"), P("dp"), P(None, "tensor"))
    return jax.shard_map(
        local,
        mesh=mesh,
        in_specs=placed,
        out_specs=(P("dp", None, "tensor"), P(None, "tensor")),
        check_vma=False,
    )
```

```python
import jax
import jax.numpy as jnp
from jax import lax
from jax.sharding import PartitionSpec as P
import jax.experimental.pallas as pl
import jax.experimental.pallas.tpu as pltpu

MESH = pl.DeviceIdType.MESH
HIGHEST = lax.Precision.HIGHEST
F32 = jnp.float32
BF16 = jnp.bfloat16
ROWS, RANK, WIDTH, REPLICAS = 768, 64, 1024, 64
HALF, BAND = ROWS // 2, WIDTH // 4
NX, NY, NZ = 4, 4, 16
NN = (((1,), (0,)), ((), ()))
NT = (((1,), (1,)), ((), ()))
PARTNERS = 43
RING4 = (2, 1, 3, 0)
RING16 = (8, 7, 9, 6, 10, 5, 11, 4, 12, 3, 13, 2, 14, 1, 15)
PLANE = tuple((i, j) for i in RING4 for j in RING4 if (i, j) != (0, 0))
WINDOW = {0: 0, 1: 1, 2: 2, 3: -1}


def split(value):
    high = value.astype(BF16)
    return high, (value - high.astype(F32)).astype(BF16)


def tall(value):
    return jnp.concatenate(split(value), axis=0)


def fold(value):
    return value[:RANK] + value[RANK:]


def left_factor(value):
    high, low = split(value)
    return jnp.concatenate([high, high, low, low], axis=1)


def right_factor(value):
    high, low = split(value)
    return jnp.concatenate([high, low, high, low], axis=0)


def dot(a, b, dims):
    return lax.dot_general(a, b, dims, preferred_element_type=F32)


def place(x, z, y, c):
    return (x * NZ + z, y * 2 + c)


def kernel(counts, q_start, grad, residual, new_residual, q_final,
           q0, g, r, out, load_sem, store_sem,
           count_x, count_z, count_sem,
           part1, core1, rows1, zs1, part2, core2, rows2, zs2, pf, p_sem,
           qs, near, far, qf, q_sem, spread_sem, elim, p_acc):
    dp = lax.axis_index("dp")
    tensor = lax.axis_index("tensor")
    x, z, y, c = dp // NZ, dp % NZ, tensor // 2, tensor % 2
    me = x * NY + y
    turn = 1 - 2 * c

    load_q = pltpu.make_async_copy(q_start, q0, load_sem.at[0])
    load_g = pltpu.make_async_copy(grad.at[0], g, load_sem.at[1])
    load_r = pltpu.make_async_copy(residual.at[0], r, load_sem.at[2])
    load_q.start()
    load_g.start()
    load_r.start()

    def at_z(k):
        return place(x, (z + k) % NZ, y, c)

    def window_z(o):
        return (z + turn * WINDOW[o] + NZ) % NZ

    def window_back(o):
        return (z - turn * WINDOW[o] + NZ) % NZ

    core_peer = place(x, z, y, 1 - c)
    barrier = pltpu.get_barrier_semaphore()

    def announce(device):
        pl.semaphore_signal(barrier, inc=1, device_id=device, device_id_type=MESH)

    for k in RING16:
        announce(at_z(k))
    for dx, dy in PLANE:
        announce(place((x + dx) % NX, z, (y + dy) % NY, c))
    for dx in (2, 1, 3):
        for dz in (2, 14, 1, 15):
            announce(place((x + dx) % NX, (z + dz) % NZ, y, c))
    announce(core_peer)

    def send(src, dst, sems, device):
        pltpu.make_async_remote_copy(
            src_ref=src, dst_ref=dst, send_sem=sems[0], recv_sem=sems[1],
            device_id=device, device_id_type=MESH,
        ).start()

    def took(ref, sem):
        pltpu.make_async_copy(ref, ref, sem).wait()

    sent = []

    def pair(sems, i):
        return sems.at[i, 0], sems.at[i, 1]

    def half_rows(h):
        return pl.ds(pl.multiple_of(h * HALF, HALF), HALF)

    def band_cols(jx):
        return pl.ds(pl.multiple_of(jx * BAND, BAND), BAND)

    def put_part(ref, h, value, offset):
        for s in range(16):
            ref[h, s, offset:offset + 4, :] = value[4 * s:4 * s + 4]

    def left_sum(step, part, core, rows, zs, own_half, finish, after_core, after_xy):
        sems = p_sem.at[step]
        send(part.at[1 - c], core, pair(sems, 0), core_peer)
        sent.append((core, sems.at[0, 0]))
        after_core()
        own_half()
        took(core, sems.at[0, 1])
        for dx, dy in PLANE:
            px, py = (x + dx) % NX, (y + dy) % NY
            slot = px * NY + py
            part[c, slot] = part[c, slot] + core[slot]
            send(part.at[c, slot], rows.at[dx * NY + dy - 1], pair(sems, 1), place(px, z, py, c))
        sent.append((rows, sems.at[1, 0]))
        after_xy()
        part[c, me] = part[c, me] + core[me]
        took(rows, sems.at[1, 1])
        zs[z] = part[c, me] + jnp.sum(rows[...], axis=0)
        for k in RING16:
            send(zs.at[z], zs.at[z], pair(sems, 2), at_z(k))
        sent.append((zs.at[pl.ds(0, 15)], sems.at[2, 0]))
        took(zs.at[pl.ds(0, 15)], sems.at[2, 1])
        pf[step, c, me] = finish(jnp.sum(zs[...], axis=0))
        for dx, dy in PLANE:
            device = place((x + dx) % NX, z, (y + dy) % NY, c)
            send(pf.at[step, c, me], pf.at[step, c, me], pair(sems, 3), device)
        sent.append((pf.at[step, c, pl.ds(0, 15)], sems.at[3, 0]))
        took(pf.at[step, c, pl.ds(0, 15)], sems.at[3, 1])
        send(pf.at[step, c], pf.at[step, c], pair(sems, 4), core_peer)
        sent.append((pf.at[step, c], sems.at[4, 0]))

    def half_of(step, h):
        return jnp.concatenate([pf[step, h, s] for s in range(16)], axis=0)

    def eliminate(first, last):
        lane = lax.broadcasted_iota(jnp.int32, (RANK, 2 * RANK), 1)
        sub = lax.broadcasted_iota(jnp.int32, (RANK, 1), 0)

        def one(j, carry):
            rows = elim[...]
            pivot = elim[pl.ds(j, 1), :]
            here = lane == (j + RANK)
            column = jnp.sum(jnp.where(here, rows, 0.0), axis=1, keepdims=True)
            diagonal = jnp.sum(jnp.where(here[:1], pivot, 0.0), axis=1, keepdims=True)
            factor = jnp.where(sub > j, column / diagonal, 0.0)
            elim[...] = rows - factor * pivot
            return carry

        lax.fori_loop(first, last, one, 0)

    def inverse():
        lane = lax.broadcasted_iota(jnp.int32, (RANK, 2 * RANK), 1)
        sub = lax.broadcasted_iota(jnp.int32, (RANK, 2 * RANK), 0)
        rows = elim[...]
        diagonal = jnp.sum(jnp.where(lane == sub + RANK, rows, 0.0), axis=1, keepdims=True)
        return rows[:, :RANK] / jnp.sqrt(diagonal)

    def right_sum(step, weight, use):
        sems = q_sem.at[step]
        own = half_of(step, c)
        plain, weighted = tall(own), tall(weight * own)
        for jx in range(NX):
            cols = slice(BAND * jx, BAND * (jx + 1))
            terms = dot(weighted, g[half_rows(c), cols], NN) + dot(plain, r[half_rows(c), cols], NN)
            qs[step, jx] = fold(terms).reshape(4, 16, BAND)
        took(pf.at[step, 1 - c], p_sem.at[step, 4, 1])
        other = half_of(step, 1 - c)
        plain, weighted = tall(other), tall(weight * other)
        for dx in RING4:
            px = (x + dx) % NX
            rows, cols = half_rows(1 - c), band_cols(px)
            terms = dot(weighted, g[rows, cols], NN) + dot(plain, r[rows, cols], NN)
            qs[step, px] = qs[step, px] + fold(terms).reshape(4, 16, BAND)
            for o in RING4:
                if (dx, o) != (0, 0):
                    pz = window_z(o)
                    send(qs.at[step, px, pz % 4], near.at[step, dx * 4 + o - 1], pair(sems, 0), place(px, pz, y, c))
        sent.append((near.at[step], sems.at[0, 0]))
        p_sum = jnp.concatenate([half_of(step, 0), half_of(step, 1)], axis=1)
        diagonal = (
            lax.broadcasted_iota(jnp.int32, (RANK, 2 * RANK), 0)
            == lax.broadcasted_iota(jnp.int32, (RANK, 2 * RANK), 1)
        )
        elim[...] = lax.dot_general(
            p_sum, jnp.concatenate([jnp.zeros_like(p_sum), p_sum], axis=0), NT,
            precision=HIGHEST, preferred_element_type=F32,
        ) + jnp.where(diagonal, 1.0, 0.0)
        eliminate(0, 28)
        took(near.at[step], sems.at[0, 1])
        block = z // 4
        far[step, block] = qs[step, x, z % 4] + jnp.sum(near[step], axis=0)
        for k in (8, 4, 12):
            send(far.at[step, block], far.at[step, block], pair(sems, 1), at_z(k))
        sent.append((far.at[step, pl.ds(0, 3)], sems.at[1, 0]))
        eliminate(28, 64)
        took(far.at[step, pl.ds(0, 3)], sems.at[1, 1])
        qf[step, x, z % 4] = jnp.sum(far[step], axis=0)
        mine = qf.at[step, x, z % 4]
        for dx in RING4:
            for o in RING4:
                if (dx, o) != (0, 0):
                    send(mine, mine, (sems.at[2, 0], spread_sem.at[step, x]), place((x + dx) % NX, window_back(o), y, c))
        for n in range(3):
            sent.append((qf.at[step, n], sems.at[2, 0]))
        sent.append((qf.at[step, 0, pl.ds(0, 3)], sems.at[2, 0]))
        use(inverse(), p_sum)

    def bands(step, inverse_left):
        for dx in (0, 1, 3, 2):
            px = (x + dx) % NX
            if dx == 0:
                took(qf.at[step, x, pl.ds(0, 3)], spread_sem.at[step, x])
            else:
                took(qf.at[step, px], spread_sem.at[step, px])
            band = qf[step, px].reshape(RANK, BAND) * (1.0 / REPLICAS)
            yield dx, band_cols(px), dot(inverse_left, right_factor(band), NN)

    tokens = counts[0].astype(F32)
    load_q.wait()
    first = tall(q0[...])
    load_g.wait()
    load_r.wait()
    for h in (0, 1):
        rows = slice(HALF * h, HALF * (h + 1))
        put_part(part1, h, fold(dot(first, g[rows], NT)) * tokens, 0)
        put_part(part1, h, fold(dot(first, r[rows], NT)), 4)
    count_x[0] = jnp.full((1, 128), tokens, F32)
    pl.semaphore_wait(barrier, PARTNERS)

    def count_to_x():
        for k in (2, 1, 3):
            send(count_x.at[0], count_x.at[k], pair(count_sem, 0), place((x + k) % NX, z, y, c))
        sent.append((count_x.at[pl.ds(1, 3)], count_sem.at[0, 0]))

    def count_to_z():
        took(count_x.at[pl.ds(1, 3)], count_sem.at[0, 1])
        count_z[z] = jnp.sum(count_x[...], axis=0)
        for k in RING16:
            send(count_z.at[z], count_z.at[z], pair(count_sem, 1), at_z(k))
        sent.append((count_z.at[pl.ds(0, 15)], count_sem.at[1, 0]))

    def finish_first(total):
        took(count_z.at[pl.ds(0, 15)], count_sem.at[1, 1])
        all_tokens = jnp.sum(count_z[...], axis=0)[:, :1]
        return (total[:4] * (REPLICAS / all_tokens) + total[4:]) * (1.0 / REPLICAS)

    nothing = lambda: None
    left_sum(0, part1, core1, rows1, zs1, nothing, finish_first, count_to_x, count_to_z)
    weight = REPLICAS * tokens / jnp.sum(count_z[...], axis=0)[:, :1]

    kept = []
    right_sum(0, weight, lambda lower_inverse, p_sum: kept.append(left_factor(lower_inverse)))
    inverse_left = kept.pop()

    def left_terms(plain, weighted, h, cols):
        rows = half_rows(h)
        return fold(dot(weighted, g[rows, cols], NT) + dot(plain, r[rows, cols], NT))

    for dx, cols, band in bands(0, inverse_left):
        plain, weighted = tall(band), tall(weight * band)
        terms = left_terms(plain, weighted, 1 - c, cols)
        if dx == 0:
            p_acc[1 - c] = terms
        elif dx != 2:
            p_acc[1 - c] = p_acc[1 - c] + terms
        else:
            put_part(part2, 1 - c, p_acc[1 - c] + terms, 0)
            break
        terms = left_terms(plain, weighted, c, cols)
        p_acc[c] = terms if dx == 0 else p_acc[c] + terms

    def own_half():
        put_part(part2, c, p_acc[c] + left_terms(plain, weighted, c, cols), 0)

    left_sum(1, part2, core2, rows2, zs2, own_half, lambda total: total * (1.0 / REPLICAS), nothing, nothing)

    def last_left(lower_inverse, p_sum):
        p_basis = lax.dot_general(lower_inverse, p_sum, NN, precision=HIGHEST, preferred_element_type=F32)
        high = p_basis.astype(BF16).astype(F32)
        low = p_basis - high
        kept.append(left_factor(lower_inverse))
        kept.append(jnp.concatenate([high, high, low, low], axis=0).T.astype(BF16))

    right_sum(1, weight, last_left)
    p_left = kept.pop()
    inverse_left = kept.pop()
    stores = []
    for dx, cols, band in bands(1, inverse_left):
        q_final[:, cols] = band
        approx = dot(p_left, right_factor(band), NN)
        matrix = weight * g[:, cols].astype(F32) + r[:, cols].astype(F32)
        out[:, cols] = (matrix - approx).astype(BF16)
        store = pltpu.make_async_copy(out.at[:, cols], new_residual.at[0, :, cols], store_sem.at[dx])
        store.start()
        stores.append(store)
    for store in stores:
        store.wait()
    for ref, sem in sent:
        took(ref, sem)


def local(grad, residual, counts, q_start):
    vmem = pl.BlockSpec(memory_space=pltpu.VMEM)
    anywhere = pl.BlockSpec(memory_space=pl.ANY)
    dma = pltpu.SemaphoreType.DMA
    return pl.pallas_call(
        kernel,
        out_shape=(
            jax.ShapeDtypeStruct((1, ROWS, WIDTH), BF16),
            jax.ShapeDtypeStruct((RANK, WIDTH), F32),
        ),
        in_specs=[pl.BlockSpec(memory_space=pltpu.SMEM), anywhere, anywhere, anywhere],
        out_specs=(anywhere, vmem),
        scratch_shapes=[
            pltpu.VMEM((RANK, WIDTH), F32),
            pltpu.VMEM((ROWS, WIDTH), BF16),
            pltpu.VMEM((ROWS, WIDTH), BF16),
            pltpu.VMEM((ROWS, WIDTH), BF16),
            dma((3,)),
            dma((4,)),
            pltpu.VMEM((4, 1, 128), F32),
            pltpu.VMEM((16, 1, 128), F32),
            dma((2, 2)),
            pltpu.VMEM((2, 16, 8, HALF), F32),
            pltpu.VMEM((16, 8, HALF), F32),
            pltpu.VMEM((15, 8, HALF), F32),
            pltpu.VMEM((16, 8, HALF), F32),
            pltpu.VMEM((2, 16, 4, HALF), F32),
            pltpu.VMEM((16, 4, HALF), F32),
            pltpu.VMEM((15, 4, HALF), F32),
            pltpu.VMEM((16, 4, HALF), F32),
            pltpu.VMEM((2, 2, 16, 4, HALF), F32),
            dma((2, 5, 2)),
            pltpu.VMEM((2, 4, 4, 16, BAND), F32),
            pltpu.VMEM((2, 15, 16, BAND), F32),
            pltpu.VMEM((2, 4, 16, BAND), F32),
            pltpu.VMEM((2, 4, 4, 16, BAND), F32),
            dma((2, 3, 2)),
            dma((2, 4)),
            pltpu.VMEM((RANK, 2 * RANK), F32),
            pltpu.VMEM((2, RANK, HALF), F32),
        ],
        compiler_params=pltpu.CompilerParams(
            collective_id=0, has_side_effects=True, vmem_limit_bytes=60 * 1024 * 1024
        ),
        name="power_step",
    )(counts, q_start, grad, residual)


def solution(mesh):
    placed = (P("dp", None, "tensor"), P("dp", None, "tensor"), P("dp"), P(None, "tensor"))
    return jax.shard_map(
        local,
        mesh=mesh,
        in_specs=placed,
        out_specs=(P("dp", None, "tensor"), P(None, "tensor")),
        check_vma=False,
    )
```

```python
import jax
import jax.numpy as jnp
from jax import lax
from jax.sharding import PartitionSpec as P
import jax.experimental.pallas as pl
import jax.experimental.pallas.tpu as pltpu

MESH = pl.DeviceIdType.MESH
HIGHEST = lax.Precision.HIGHEST
F32 = jnp.float32
BF16 = jnp.bfloat16
ROWS, RANK, WIDTH, REPLICAS = 768, 64, 1024, 64
HALF, BAND = ROWS // 2, WIDTH // 4
NX, NY, NZ = 4, 4, 16
NN = (((1,), (0,)), ((), ()))
NT = (((1,), (1,)), ((), ()))
PARTNERS = 58
RING4 = (2, 1, 3, 0)
RING16 = (8, 7, 9, 6, 10, 5, 11, 4, 12, 3, 13, 2, 14, 1, 15)
PLANE = tuple((i, j) for i in RING4 for j in RING4)
WINDOW = {0: 0, 1: 1, 2: 2, 3: -1}


def split(value):
    high = value.astype(BF16)
    return high, (value - high.astype(F32)).astype(BF16)


def tall(value):
    return jnp.concatenate(split(value), axis=0)


def fold(value):
    return value[:RANK] + value[RANK:]


def left_factor(value):
    high, low = split(value)
    return jnp.concatenate([high, high, low, low], axis=1)


def right_factor(value):
    high, low = split(value)
    return jnp.concatenate([high, low, high, low], axis=0)


def dot(a, b, dims):
    return lax.dot_general(a, b, dims, preferred_element_type=F32)


def place(x, z, y, c):
    return (x * NZ + z, y * 2 + c)


def kernel(counts, q_start, grad, residual, new_residual, q_final,
           q0, g, r, load_sem,
           count_x, count_z, count_sem,
           part1, rows1, zs1, part2, rows2, zs2, pf, p_sem,
           qs, near, far, qf, q_sem, spread_sem, elim, p_acc):
    dp = lax.axis_index("dp")
    tensor = lax.axis_index("tensor")
    x, z, y, c = dp // NZ, dp % NZ, tensor // 2, tensor % 2
    me = x * NY + y
    turn = 1 - 2 * c

    load_q = pltpu.make_async_copy(q_start, q0, load_sem.at[0])
    load_g = pltpu.make_async_copy(grad.at[0], g, load_sem.at[1])
    load_r = pltpu.make_async_copy(residual.at[0], r, load_sem.at[2])
    load_q.start()
    load_g.start()
    load_r.start()

    def at_z(k):
        return place(x, (z + k) % NZ, y, c)

    def window_z(o):
        return (z + turn * WINDOW[o] + NZ) % NZ

    def window_back(o):
        return (z - turn * WINDOW[o] + NZ) % NZ

    barrier = pltpu.get_barrier_semaphore()

    def announce(device):
        pl.semaphore_signal(barrier, inc=1, device_id=device, device_id_type=MESH)

    for k in RING16:
        announce(at_z(k))
    for dx, dy in PLANE:
        for core in (1, 0):
            if (dx, dy, core) != (0, 0, 0):
                announce(place((x + dx) % NX, z, (y + dy) % NY, (c + core) % 2))
    for dx in (2, 1, 3):
        for dz in (2, 14, 1, 15):
            announce(place((x + dx) % NX, (z + dz) % NZ, y, c))

    def send(src, dst, sems, device):
        pltpu.make_async_remote_copy(
            src_ref=src, dst_ref=dst, send_sem=sems[0], recv_sem=sems[1],
            device_id=device, device_id_type=MESH,
        ).start()

    def took(ref, sem):
        pltpu.make_async_copy(ref, ref, sem).wait()

    sent = []

    def pair(sems, i):
        return sems.at[i, 0], sems.at[i, 1]

    def half_rows(h):
        return pl.ds(pl.multiple_of(h * HALF, HALF), HALF)

    def band_cols(jx):
        return pl.ds(pl.multiple_of(jx * BAND, BAND), BAND)

    def put_part(ref, h, value, offset):
        for s in range(16):
            ref[h, s, offset:offset + 4, :] = value[4 * s:4 * s + 4]

    def left_sum(step, part, rows, zs, own_half, finish, after_send):
        sems = p_sem.at[step]
        for core in (1, 0):
            half = (c + core) % 2
            for dx, dy in PLANE:
                if (dx, dy, core) != (0, 0, 0):
                    px, py = (x + dx) % NX, (y + dy) % NY
                    slot = 16 * core + 4 * dx + dy - 1
                    send(part.at[half, px * NY + py], rows.at[slot], pair(sems, 0), place(px, z, py, half))
            if core == 1:
                own_half()
        sent.append((rows, sems.at[0, 0]))
        after_send()
        took(rows, sems.at[0, 1])
        zs[z] = part[c, me] + jnp.sum(rows[...], axis=0)
        for k in RING16:
            send(zs.at[z], zs.at[z], pair(sems, 1), at_z(k))
        sent.append((zs.at[pl.ds(0, 15)], sems.at[1, 0]))
        took(zs.at[pl.ds(0, 15)], sems.at[1, 1])
        pf[step, c, me] = finish(jnp.sum(zs[...], axis=0))
        mine = pf.at[step, c, me]
        for core in (1, 0):
            for dx, dy in PLANE:
                if (dx, dy, core) != (0, 0, 0):
                    device = place((x + dx) % NX, z, (y + dy) % NY, (c + core) % 2)
                    send(mine, mine, (sems.at[2 + core, 0], sems.at[2 + core, 1]), device)
        sent.append((pf.at[step, c, pl.ds(0, 15)], sems.at[2, 0]))
        sent.append((pf.at[step, c], sems.at[3, 0]))
        took(pf.at[step, c, pl.ds(0, 15)], sems.at[2, 1])

    def half_of(step, h):
        return jnp.concatenate([pf[step, h, s] for s in range(16)], axis=0)

    def eliminate(first, last):
        lane = lax.broadcasted_iota(jnp.int32, (RANK, 2 * RANK), 1)
        sub = lax.broadcasted_iota(jnp.int32, (RANK, 1), 0)

        def one(j, carry):
            rows = elim[...]
            pivot = elim[pl.ds(j, 1), :]
            here = lane == (j + RANK)
            column = jnp.sum(jnp.where(here, rows, 0.0), axis=1, keepdims=True)
            diagonal = jnp.sum(jnp.where(here[:1], pivot, 0.0), axis=1, keepdims=True)
            factor = jnp.where(sub > j, column / diagonal, 0.0)
            elim[...] = rows - factor * pivot
            return carry

        lax.fori_loop(first, last, one, 0)

    def inverse():
        lane = lax.broadcasted_iota(jnp.int32, (RANK, 2 * RANK), 1)
        sub = lax.broadcasted_iota(jnp.int32, (RANK, 2 * RANK), 0)
        rows = elim[...]
        diagonal = jnp.sum(jnp.where(lane == sub + RANK, rows, 0.0), axis=1, keepdims=True)
        return rows[:, :RANK] / jnp.sqrt(diagonal)

    def right_sum(step, weight, use):
        sems = q_sem.at[step]
        own = half_of(step, c)
        plain, weighted = tall(own), tall(weight * own)
        for jx in range(NX):
            cols = slice(BAND * jx, BAND * (jx + 1))
            terms = dot(weighted, g[half_rows(c), cols], NN) + dot(plain, r[half_rows(c), cols], NN)
            qs[step, jx] = fold(terms).reshape(4, 16, BAND)
        took(pf.at[step, 1 - c], p_sem.at[step, 3, 1])
        other = half_of(step, 1 - c)
        plain, weighted = tall(other), tall(weight * other)
        for dx in RING4:
            px = (x + dx) % NX
            rows, cols = half_rows(1 - c), band_cols(px)
            terms = dot(weighted, g[rows, cols], NN) + dot(plain, r[rows, cols], NN)
            qs[step, px] = qs[step, px] + fold(terms).reshape(4, 16, BAND)
            for o in RING4:
                if (dx, o) != (0, 0):
                    pz = window_z(o)
                    send(qs.at[step, px, pz % 4], near.at[step, dx * 4 + o - 1], pair(sems, 0), place(px, pz, y, c))
        sent.append((near.at[step], sems.at[0, 0]))
        p_sum = jnp.concatenate([half_of(step, 0), half_of(step, 1)], axis=1)
        diagonal = (
            lax.broadcasted_iota(jnp.int32, (RANK, 2 * RANK), 0)
            == lax.broadcasted_iota(jnp.int32, (RANK, 2 * RANK), 1)
        )
        elim[...] = lax.dot_general(
            p_sum, jnp.concatenate([jnp.zeros_like(p_sum), p_sum], axis=0), NT,
            precision=HIGHEST, preferred_element_type=F32,
        ) + jnp.where(diagonal, 1.0, 0.0)
        eliminate(0, 28)
        took(near.at[step], sems.at[0, 1])
        block = z // 4
        far[step, block] = qs[step, x, z % 4] + jnp.sum(near[step], axis=0)
        for k in (8, 4, 12):
            send(far.at[step, block], far.at[step, block], pair(sems, 1), at_z(k))
        sent.append((far.at[step, pl.ds(0, 3)], sems.at[1, 0]))
        eliminate(28, 64)
        took(far.at[step, pl.ds(0, 3)], sems.at[1, 1])
        qf[step, x, z % 4] = jnp.sum(far[step], axis=0)
        mine = qf.at[step, x, z % 4]
        for dx in RING4:
            for o in RING4:
                if (dx, o) != (0, 0):
                    send(mine, mine, (sems.at[2, 0], spread_sem.at[step, x]), place((x + dx) % NX, window_back(o), y, c))
        for n in range(3):
            sent.append((qf.at[step, n], sems.at[2, 0]))
        sent.append((qf.at[step, 0, pl.ds(0, 3)], sems.at[2, 0]))
        use(inverse(), p_sum)

    def bands(step, inverse_left):
        for dx in (0, 1, 3, 2):
            px = (x + dx) % NX
            if dx == 0:
                took(qf.at[step, x, pl.ds(0, 3)], spread_sem.at[step, x])
            else:
                took(qf.at[step, px], spread_sem.at[step, px])
            band = qf[step, px].reshape(RANK, BAND) * (1.0 / REPLICAS)
            yield dx, band_cols(px), dot(inverse_left, right_factor(band), NN)

    tokens = counts[0].astype(F32)
    load_q.wait()
    first = tall(q0[...])
    load_g.wait()
    load_r.wait()
    for h in (0, 1):
        rows = slice(HALF * h, HALF * (h + 1))
        put_part(part1, h, fold(dot(first, g[rows], NT)) * tokens, 0)
        put_part(part1, h, fold(dot(first, r[rows], NT)), 4)
    count_x[0] = jnp.full((1, 128), tokens, F32)
    pl.semaphore_wait(barrier, PARTNERS)

    for k in (2, 1, 3):
        send(count_x.at[0], count_x.at[k], pair(count_sem, 0), place((x + k) % NX, z, y, c))
    sent.append((count_x.at[pl.ds(1, 3)], count_sem.at[0, 0]))

    def count_to_z():
        took(count_x.at[pl.ds(1, 3)], count_sem.at[0, 1])
        count_z[z] = jnp.sum(count_x[...], axis=0)
        for k in RING16:
            send(count_z.at[z], count_z.at[z], pair(count_sem, 1), at_z(k))
        sent.append((count_z.at[pl.ds(0, 15)], count_sem.at[1, 0]))

    def finish_first(total):
        took(count_z.at[pl.ds(0, 15)], count_sem.at[1, 1])
        all_tokens = jnp.sum(count_z[...], axis=0)[:, :1]
        return (total[:4] * (REPLICAS / all_tokens) + total[4:]) * (1.0 / REPLICAS)

    nothing = lambda: None
    left_sum(0, part1, rows1, zs1, nothing, finish_first, count_to_z)
    weight = REPLICAS * tokens / jnp.sum(count_z[...], axis=0)[:, :1]

    kept = []
    right_sum(0, weight, lambda lower_inverse, p_sum: kept.append(left_factor(lower_inverse)))
    inverse_left = kept.pop()

    def left_terms(plain, weighted, h, cols):
        rows = half_rows(h)
        return fold(dot(weighted, g[rows, cols], NT) + dot(plain, r[rows, cols], NT))

    for dx, cols, band in bands(0, inverse_left):
        plain, weighted = tall(band), tall(weight * band)
        terms = left_terms(plain, weighted, 1 - c, cols)
        if dx == 0:
            p_acc[1 - c] = terms
        elif dx != 2:
            p_acc[1 - c] = p_acc[1 - c] + terms
        else:
            put_part(part2, 1 - c, p_acc[1 - c] + terms, 0)
            break
        terms = left_terms(plain, weighted, c, cols)
        p_acc[c] = terms if dx == 0 else p_acc[c] + terms

    def own_half():
        put_part(part2, c, p_acc[c] + left_terms(plain, weighted, c, cols), 0)

    left_sum(1, part2, rows2, zs2, own_half, lambda total: total * (1.0 / REPLICAS), nothing)

    def last_left(lower_inverse, p_sum):
        p_basis = lax.dot_general(lower_inverse, p_sum, NN, precision=HIGHEST, preferred_element_type=F32)
        high = p_basis.astype(BF16).astype(F32)
        low = p_basis - high
        kept.append(left_factor(lower_inverse))
        kept.append(jnp.concatenate([high, high, low, low], axis=0).T.astype(BF16))

    right_sum(1, weight, last_left)
    p_left = kept.pop()
    inverse_left = kept.pop()
    for dx, cols, band in bands(1, inverse_left):
        q_final[:, cols] = band
        approx = dot(p_left, right_factor(band), NN)
        matrix = weight * g[:, cols].astype(F32) + r[:, cols].astype(F32)
        new_residual[0, :, cols] = (matrix - approx).astype(BF16)
    for ref, sem in sent:
        took(ref, sem)


def local(grad, residual, counts, q_start):
    vmem = pl.BlockSpec(memory_space=pltpu.VMEM)
    hbm = pl.BlockSpec(memory_space=pltpu.HBM)
    dma = pltpu.SemaphoreType.DMA
    return pl.pallas_call(
        kernel,
        out_shape=(
            jax.ShapeDtypeStruct((1, ROWS, WIDTH), BF16),
            jax.ShapeDtypeStruct((RANK, WIDTH), F32),
        ),
        in_specs=[pl.BlockSpec(memory_space=pltpu.SMEM), hbm, hbm, hbm],
        out_specs=(vmem, vmem),
        scratch_shapes=[
            pltpu.VMEM((RANK, WIDTH), F32),
            pltpu.VMEM((ROWS, WIDTH), BF16),
            pltpu.VMEM((ROWS, WIDTH), BF16),
            dma((3,)),
            pltpu.VMEM((4, 1, 128), F32),
            pltpu.VMEM((16, 1, 128), F32),
            dma((2, 2)),
            pltpu.VMEM((2, 16, 8, HALF), F32),
            pltpu.VMEM((31, 8, HALF), F32),
            pltpu.VMEM((16, 8, HALF), F32),
            pltpu.VMEM((2, 16, 4, HALF), F32),
            pltpu.VMEM((31, 4, HALF), F32),
            pltpu.VMEM((16, 4, HALF), F32),
            pltpu.VMEM((2, 2, 16, 4, HALF), F32),
            dma((2, 4, 2)),
            pltpu.VMEM((2, 4, 4, 16, BAND), F32),
            pltpu.VMEM((2, 15, 16, BAND), F32),
            pltpu.VMEM((2, 4, 16, BAND), F32),
            pltpu.VMEM((2, 4, 4, 16, BAND), F32),
            dma((2, 3, 2)),
            dma((2, 4)),
            pltpu.VMEM((RANK, 2 * RANK), F32),
            pltpu.VMEM((2, RANK, HALF), F32),
        ],
        compiler_params=pltpu.CompilerParams(
            collective_id=0, has_side_effects=True, vmem_limit_bytes=32 * 1024 * 1024
        ),
        name="power_step",
    )(counts, *(pltpu.with_memory_space_constraint(a, pltpu.HBM) for a in (q_start, grad, residual)))


def solution(mesh):
    placed = (P("dp", None, "tensor"), P("dp", None, "tensor"), P("dp"), P(None, "tensor"))
    return jax.shard_map(
        local,
        mesh=mesh,
        in_specs=placed,
        out_specs=(P("dp", None, "tensor"), P(None, "tensor")),
        check_vma=False,
    )
```

```python
import jax
import jax.numpy as jnp
from jax import lax
from jax.sharding import PartitionSpec as P
import jax.experimental.pallas as pl
import jax.experimental.pallas.tpu as pltpu

MESH = pl.DeviceIdType.MESH
HIGHEST = lax.Precision.HIGHEST
F32 = jnp.float32
BF16 = jnp.bfloat16
ROWS, RANK, WIDTH, REPLICAS = 768, 64, 1024, 64
HALF, BAND = ROWS // 2, WIDTH // 4
NX, NY, NZ = 4, 4, 16
NN = (((1,), (0,)), ((), ()))
NT = (((1,), (1,)), ((), ()))
PARTNERS = 58
RING4 = (2, 1, 3, 0)
RING16 = (8, 7, 9, 6, 10, 5, 11, 4, 12, 3, 13, 2, 14, 1, 15)
PLANE = tuple((i, j) for i in RING4 for j in RING4)
WINDOW = {0: 0, 1: 1, 2: 2, 3: -1}


def split(value):
    high = value.astype(BF16)
    return high, (value - high.astype(F32)).astype(BF16)


def tall(value):
    return jnp.concatenate(split(value), axis=0)


def fold(value):
    return value[:RANK] + value[RANK:]


def left_factor(value):
    high, low = split(value)
    return jnp.concatenate([high, high, low, low], axis=1)


def right_factor(value):
    high, low = split(value)
    return jnp.concatenate([high, low, high, low], axis=0)


def dot(a, b, dims):
    return lax.dot_general(a, b, dims, preferred_element_type=F32)


def place(x, z, y, c):
    return (x * NZ + z, y * 2 + c)


def kernel(counts, q_start, grad, residual, new_residual, q_final,
           q0, g, r, load_sem,
           count_x, count_z, count_sem,
           part1, rows1, zs1, part2, rows2, zs2, pf, p_sem,
           qs, near, far, qf, q_sem, spread_sem, elim, p_acc):
    dp = lax.axis_index("dp")
    tensor = lax.axis_index("tensor")
    x, z, y, c = dp // NZ, dp % NZ, tensor // 2, tensor % 2
    me = x * NY + y
    turn = 1 - 2 * c

    load_q = pltpu.make_async_copy(q_start, q0, load_sem.at[0])
    load_g = pltpu.make_async_copy(grad.at[0], g, load_sem.at[1])
    load_r = pltpu.make_async_copy(residual.at[0], r, load_sem.at[2])
    load_q.start()
    load_g.start()
    load_r.start()

    def at_z(k):
        return place(x, (z + k) % NZ, y, c)

    def window_z(o):
        return (z + turn * WINDOW[o] + NZ) % NZ

    def window_back(o):
        return (z - turn * WINDOW[o] + NZ) % NZ

    barrier = pltpu.get_barrier_semaphore()

    def announce(device):
        pl.semaphore_signal(barrier, inc=1, device_id=device, device_id_type=MESH)

    for k in RING16:
        announce(at_z(k))
    for dx, dy in PLANE:
        for core in (1, 0):
            if (dx, dy, core) != (0, 0, 0):
                announce(place((x + dx) % NX, z, (y + dy) % NY, (c + core) % 2))
    for dx in (2, 1, 3):
        for dz in (2, 14, 1, 15):
            announce(place((x + dx) % NX, (z + dz) % NZ, y, c))

    def send(src, dst, sems, device):
        pltpu.make_async_remote_copy(
            src_ref=src, dst_ref=dst, send_sem=sems[0], recv_sem=sems[1],
            device_id=device, device_id_type=MESH,
        ).start()

    def took(ref, sem):
        pltpu.make_async_copy(ref, ref, sem).wait()

    sent = []

    def pair(sems, i):
        return sems.at[i, 0], sems.at[i, 1]

    def half_rows(h):
        return pl.ds(pl.multiple_of(h * HALF, HALF), HALF)

    def band_cols(jx):
        return pl.ds(pl.multiple_of(jx * BAND, BAND), BAND)

    def put_part(ref, h, value, offset):
        for s in range(16):
            ref[h, s, offset:offset + 4, :] = value[4 * s:4 * s + 4]

    def left_sum(step, part, rows, zs, own_half, finish, after_send):
        sems = p_sem.at[step]
        for core in (1, 0):
            half = (c + core) % 2
            for dx, dy in PLANE:
                if (dx, dy, core) != (0, 0, 0):
                    px, py = (x + dx) % NX, (y + dy) % NY
                    slot = 16 * core + 4 * dx + dy - 1
                    send(part.at[half, px * NY + py], rows.at[slot], pair(sems, 0), place(px, z, py, half))
            if core == 1:
                own_half()
        sent.append((rows, sems.at[0, 0]))
        after_send()
        took(rows, sems.at[0, 1])
        zs[z] = part[c, me] + jnp.sum(rows[...], axis=0)
        for k in RING16:
            send(zs.at[z], zs.at[z], pair(sems, 1), at_z(k))
        sent.append((zs.at[pl.ds(0, 15)], sems.at[1, 0]))
        took(zs.at[pl.ds(0, 15)], sems.at[1, 1])
        pf[step, c, me] = finish(jnp.sum(zs[...], axis=0))
        mine = pf.at[step, c, me]
        for core in (1, 0):
            for dx, dy in PLANE:
                if (dx, dy, core) != (0, 0, 0):
                    device = place((x + dx) % NX, z, (y + dy) % NY, (c + core) % 2)
                    send(mine, mine, (sems.at[2 + core, 0], sems.at[2 + core, 1]), device)
        sent.append((pf.at[step, c, pl.ds(0, 15)], sems.at[2, 0]))
        sent.append((pf.at[step, c], sems.at[3, 0]))
        took(pf.at[step, c, pl.ds(0, 15)], sems.at[2, 1])

    def half_of(step, h):
        return jnp.concatenate([pf[step, h, s] for s in range(16)], axis=0)

    def eliminate(first, last):
        lane = lax.broadcasted_iota(jnp.int32, (RANK, 2 * RANK), 1)
        sub = lax.broadcasted_iota(jnp.int32, (RANK, 1), 0)

        def one(j, carry):
            rows = elim[...]
            pivot = elim[pl.ds(j, 1), :]
            here = lane == (j + RANK)
            column = jnp.sum(jnp.where(here, rows, 0.0), axis=1, keepdims=True)
            diagonal = jnp.sum(jnp.where(here[:1], pivot, 0.0), axis=1, keepdims=True)
            factor = jnp.where(sub > j, column / diagonal, 0.0)
            elim[...] = rows - factor * pivot
            return carry

        lax.fori_loop(first, last, one, 0)

    def inverse():
        lane = lax.broadcasted_iota(jnp.int32, (RANK, 2 * RANK), 1)
        sub = lax.broadcasted_iota(jnp.int32, (RANK, 2 * RANK), 0)
        rows = elim[...]
        diagonal = jnp.sum(jnp.where(lane == sub + RANK, rows, 0.0), axis=1, keepdims=True)
        return rows[:, :RANK] / jnp.sqrt(diagonal)

    def right_sum(step, weight, use):
        sems = q_sem.at[step]
        took(pf.at[step, 1 - c], p_sem.at[step, 3, 1])
        p_sum = jnp.concatenate([half_of(step, 0), half_of(step, 1)], axis=1)
        plain, weighted = tall(p_sum), tall(weight * p_sum)
        for dx in RING4:
            px = (x + dx) % NX
            cols = band_cols(px)
            terms = dot(weighted, g[:, cols], NN) + dot(plain, r[:, cols], NN)
            qs[step, px] = fold(terms).reshape(4, 16, BAND)
            for o in RING4:
                if (dx, o) != (0, 0):
                    pz = window_z(o)
                    send(qs.at[step, px, pz % 4], near.at[step, dx * 4 + o - 1], pair(sems, 0), place(px, pz, y, c))
        sent.append((near.at[step], sems.at[0, 0]))
        diagonal = (
            lax.broadcasted_iota(jnp.int32, (RANK, 2 * RANK), 0)
            == lax.broadcasted_iota(jnp.int32, (RANK, 2 * RANK), 1)
        )
        elim[...] = lax.dot_general(
            p_sum, jnp.concatenate([jnp.zeros_like(p_sum), p_sum], axis=0), NT,
            precision=HIGHEST, preferred_element_type=F32,
        ) + jnp.where(diagonal, 1.0, 0.0)
        eliminate(0, 28)
        took(near.at[step], sems.at[0, 1])
        block = z // 4
        far[step, block] = qs[step, x, z % 4] + jnp.sum(near[step], axis=0)
        for k in (8, 4, 12):
            send(far.at[step, block], far.at[step, block], pair(sems, 1), at_z(k))
        sent.append((far.at[step, pl.ds(0, 3)], sems.at[1, 0]))
        eliminate(28, 64)
        took(far.at[step, pl.ds(0, 3)], sems.at[1, 1])
        qf[step, x, z % 4] = jnp.sum(far[step], axis=0)
        mine = qf.at[step, x, z % 4]
        for dx in RING4:
            for o in RING4:
                if (dx, o) != (0, 0):
                    send(mine, mine, (sems.at[2, 0], spread_sem.at[step, x]), place((x + dx) % NX, window_back(o), y, c))
        for n in range(3):
            sent.append((qf.at[step, n], sems.at[2, 0]))
        sent.append((qf.at[step, 0, pl.ds(0, 3)], sems.at[2, 0]))
        use(inverse(), p_sum)

    def bands(step, inverse_left):
        for dx in (0, 1, 3, 2):
            px = (x + dx) % NX
            if dx == 0:
                took(qf.at[step, x, pl.ds(0, 3)], spread_sem.at[step, x])
            else:
                took(qf.at[step, px], spread_sem.at[step, px])
            band = qf[step, px].reshape(RANK, BAND) * (1.0 / REPLICAS)
            yield dx, band_cols(px), dot(inverse_left, right_factor(band), NN)

    tokens = counts[0].astype(F32)
    load_q.wait()
    first = tall(q0[...])
    load_g.wait()
    load_r.wait()
    for h in (0, 1):
        rows = slice(HALF * h, HALF * (h + 1))
        put_part(part1, h, fold(dot(first, g[rows], NT)) * tokens, 0)
        put_part(part1, h, fold(dot(first, r[rows], NT)), 4)
    count_x[0] = jnp.full((1, 128), tokens, F32)
    pl.semaphore_wait(barrier, PARTNERS)

    for k in (2, 1, 3):
        send(count_x.at[0], count_x.at[k], pair(count_sem, 0), place((x + k) % NX, z, y, c))
    sent.append((count_x.at[pl.ds(1, 3)], count_sem.at[0, 0]))

    def count_to_z():
        took(count_x.at[pl.ds(1, 3)], count_sem.at[0, 1])
        count_z[z] = jnp.sum(count_x[...], axis=0)
        for k in RING16:
            send(count_z.at[z], count_z.at[z], pair(count_sem, 1), at_z(k))
        sent.append((count_z.at[pl.ds(0, 15)], count_sem.at[1, 0]))

    def finish_first(total):
        took(count_z.at[pl.ds(0, 15)], count_sem.at[1, 1])
        all_tokens = jnp.sum(count_z[...], axis=0)[:, :1]
        return (total[:4] * (REPLICAS / all_tokens) + total[4:]) * (1.0 / REPLICAS)

    nothing = lambda: None
    left_sum(0, part1, rows1, zs1, nothing, finish_first, count_to_z)
    weight = REPLICAS * tokens / jnp.sum(count_z[...], axis=0)[:, :1]

    kept = []
    right_sum(0, weight, lambda lower_inverse, p_sum: kept.append(left_factor(lower_inverse)))
    inverse_left = kept.pop()

    def left_terms(plain, weighted, rows, cols):
        return fold(dot(weighted, g[rows, cols], NT) + dot(plain, r[rows, cols], NT))

    for dx, cols, band in bands(0, inverse_left):
        plain, weighted = tall(band), tall(weight * band)
        if dx == 0:
            p_acc[...] = left_terms(plain, weighted, slice(None), cols)
        elif dx != 2:
            p_acc[...] = p_acc[...] + left_terms(plain, weighted, slice(None), cols)
    last = cols

    def put_half(h):
        terms = left_terms(plain, weighted, half_rows(h), last)
        put_part(part2, h, p_acc[:, half_rows(h)] + terms, 0)

    put_half(1 - c)

    def own_half():
        put_half(c)

    left_sum(1, part2, rows2, zs2, own_half, lambda total: total * (1.0 / REPLICAS), nothing)

    def last_left(lower_inverse, p_sum):
        p_basis = lax.dot_general(lower_inverse, p_sum, NN, precision=HIGHEST, preferred_element_type=F32)
        high = p_basis.astype(BF16).astype(F32)
        low = p_basis - high
        kept.append(left_factor(lower_inverse))
        kept.append(jnp.concatenate([high, high, low, low], axis=0).T.astype(BF16))
        while len(sent) > 4:
            took(*sent.pop(0))

    right_sum(1, weight, last_left)
    p_left = kept.pop()
    inverse_left = kept.pop()
    for dx, cols, band in bands(1, inverse_left):
        q_final[:, cols] = band
        approx = dot(p_left, right_factor(band), NN)
        matrix = weight * g[:, cols].astype(F32) + r[:, cols].astype(F32)
        new_residual[0, :, cols] = (matrix - approx).astype(BF16)
    for ref, sem in sent:
        took(ref, sem)


def store(residual_in, q_in, residual_out, q_out, sems):
    copies = [
        pltpu.make_async_copy(residual_in, residual_out, sems.at[0]),
        pltpu.make_async_copy(q_in, q_out, sems.at[1]),
    ]
    for copy in copies:
        copy.start()
    for copy in copies:
        copy.wait()


def local(grad, residual, counts, q_start):
    vmem = pl.BlockSpec(memory_space=pltpu.VMEM)
    hbm = pl.BlockSpec(memory_space=pltpu.HBM)
    dma = pltpu.SemaphoreType.DMA
    operands = [pltpu.with_memory_space_constraint(a, pltpu.HBM) for a in (q_start, grad, residual)]
    results = pl.pallas_call(
        kernel,
        out_shape=(
            jax.ShapeDtypeStruct((1, ROWS, WIDTH), BF16),
            jax.ShapeDtypeStruct((RANK, WIDTH), F32),
        ),
        in_specs=[pl.BlockSpec(memory_space=pltpu.SMEM), hbm, hbm, hbm],
        out_specs=(vmem, vmem),
        scratch_shapes=[
            pltpu.VMEM((RANK, WIDTH), F32),
            pltpu.VMEM((ROWS, WIDTH), BF16),
            pltpu.VMEM((ROWS, WIDTH), BF16),
            dma((3,)),
            pltpu.VMEM((4, 1, 128), F32),
            pltpu.VMEM((16, 1, 128), F32),
            dma((2, 2)),
            pltpu.VMEM((2, 16, 8, HALF), F32),
            pltpu.VMEM((31, 8, HALF), F32),
            pltpu.VMEM((16, 8, HALF), F32),
            pltpu.VMEM((2, 16, 4, HALF), F32),
            pltpu.VMEM((31, 4, HALF), F32),
            pltpu.VMEM((16, 4, HALF), F32),
            pltpu.VMEM((2, 2, 16, 4, HALF), F32),
            dma((2, 4, 2)),
            pltpu.VMEM((2, 4, 4, 16, BAND), F32),
            pltpu.VMEM((2, 15, 16, BAND), F32),
            pltpu.VMEM((2, 4, 16, BAND), F32),
            pltpu.VMEM((2, 4, 4, 16, BAND), F32),
            dma((2, 3, 2)),
            dma((2, 4)),
            pltpu.VMEM((RANK, 2 * RANK), F32),
            pltpu.VMEM((RANK, ROWS), F32),
        ],
        compiler_params=pltpu.CompilerParams(
            collective_id=0, has_side_effects=True, vmem_limit_bytes=32 * 1024 * 1024
        ),
        name="power_step",
    )(counts, *operands)
    return pl.pallas_call(
        store,
        out_shape=(
            jax.ShapeDtypeStruct((1, ROWS, WIDTH), BF16),
            jax.ShapeDtypeStruct((RANK, WIDTH), F32),
        ),
        in_specs=[vmem, vmem],
        out_specs=(hbm, hbm),
        scratch_shapes=[dma((2,))],
        name="store",
    )(*(pltpu.with_memory_space_constraint(a, pltpu.VMEM) for a in results))


def solution(mesh):
    placed = (P("dp", None, "tensor"), P("dp", None, "tensor"), P("dp"), P(None, "tensor"))
    return jax.shard_map(
        local,
        mesh=mesh,
        in_specs=placed,
        out_specs=(P("dp", None, "tensor"), P(None, "tensor")),
        check_vma=False,
    )
```

```python
import jax
import jax.numpy as jnp
from jax import lax
from jax.sharding import PartitionSpec as P
import jax.experimental.pallas as pl
import jax.experimental.pallas.tpu as pltpu

MESH = pl.DeviceIdType.MESH
HIGHEST = lax.Precision.HIGHEST
F32 = jnp.float32
BF16 = jnp.bfloat16
ROWS, RANK, WIDTH, REPLICAS = 768, 64, 1024, 64
HALF, BAND = ROWS // 2, WIDTH // 4
NX, NY, NZ = 4, 4, 16
NN = (((1,), (0,)), ((), ()))
NT = (((1,), (1,)), ((), ()))
PARTNERS = 51
RING4 = (2, 1, 3, 0)
RING16 = (8, 7, 9, 6, 10, 5, 11, 4, 12, 3, 13, 2, 14, 1, 15)
PLANE = tuple((i, j) for i in RING4 for j in RING4)
WINDOW = {0: 0, 1: 1, 2: 2, 3: -1}


def split(value):
    high = value.astype(BF16)
    return high, (value - high.astype(F32)).astype(BF16)


def tall(value):
    return jnp.concatenate(split(value), axis=0)


def fold(value):
    return value[:RANK] + value[RANK:]


def left_factor(value):
    high, low = split(value)
    return jnp.concatenate([high, high, low, low], axis=1)


def right_factor(value):
    high, low = split(value)
    return jnp.concatenate([high, low, high, low], axis=0)


def dot(a, b, dims):
    return lax.dot_general(a, b, dims, preferred_element_type=F32)


def place(x, z, y, c):
    return (x * NZ + z, y * 2 + c)


def kernel(counts, q_start, grad, residual, new_residual, q_final,
           q0, g, r, load_sem,
           count_x, count_z, count_sem,
           part1, rows1, zs1, part2, rows2, zs2, pf, p_sem,
           qs, near, far, qf, q_sem, spread_sem, elim, p_acc, relay):
    dp = lax.axis_index("dp")
    tensor = lax.axis_index("tensor")
    x, z, y, c = dp // NZ, dp % NZ, tensor // 2, tensor % 2
    me = x * NY + y
    turn = 1 - 2 * c

    load_q = pltpu.make_async_copy(q_start, q0, load_sem.at[0])
    load_g = pltpu.make_async_copy(grad.at[0], g, load_sem.at[1])
    load_r = pltpu.make_async_copy(residual.at[0], r, load_sem.at[2])
    load_q.start()
    load_g.start()
    load_r.start()

    def at_z(k):
        return place(x, (z + k) % NZ, y, c)

    def window_z(o):
        return (z + turn * WINDOW[o] + NZ) % NZ

    def window_back(o):
        return (z - turn * WINDOW[o] + NZ) % NZ

    barrier = pltpu.get_barrier_semaphore()

    def announce(device):
        pl.semaphore_signal(barrier, inc=1, device_id=device, device_id_type=MESH)

    for k in (4, 12, 3, 13, 2, 14, 1, 15):
        announce(at_z(k))
    for dx, dy in PLANE:
        for core in (1, 0):
            if (dx, dy, core) != (0, 0, 0):
                announce(place((x + dx) % NX, z, (y + dy) % NY, (c + core) % 2))
    for dx in (2, 1, 3):
        for dz in (2, 14, 1, 15):
            announce(place((x + dx) % NX, (z + dz) % NZ, y, c))

    def send(src, dst, sems, device):
        pltpu.make_async_remote_copy(
            src_ref=src, dst_ref=dst, send_sem=sems[0], recv_sem=sems[1],
            device_id=device, device_id_type=MESH,
        ).start()

    def took(ref, sem):
        pltpu.make_async_copy(ref, ref, sem).wait()

    sent = []

    def pair(sems, i):
        return sems.at[i, 0], sems.at[i, 1]

    def half_rows(h):
        return pl.ds(pl.multiple_of(h * HALF, HALF), HALF)

    def band_cols(jx):
        return pl.ds(pl.multiple_of(jx * BAND, BAND), BAND)

    def put_part(ref, h, value, offset):
        for s in range(16):
            ref[h, s, offset:offset + 4, :] = value[4 * s:4 * s + 4]

    def left_sum(step, part, rows, zs, own_half, finish, after_send):
        sems = p_sem.at[step]
        for core in (1, 0):
            half = (c + core) % 2
            for dx, dy in PLANE:
                if (dx, dy, core) != (0, 0, 0):
                    px, py = (x + dx) % NX, (y + dy) % NY
                    slot = 16 * core + 4 * dx + dy - 1
                    send(part.at[half, px * NY + py], rows.at[slot], pair(sems, 0), place(px, z, py, half))
            if core == 1:
                own_half()
        sent.append((rows, sems.at[0, 0]))
        after_send()
        took(rows, sems.at[0, 1])
        zs[z] = part[c, me] + jnp.sum(rows[...], axis=0)
        for k in RING16:
            send(zs.at[z], zs.at[z], pair(sems, 1), at_z(k))
        sent.append((zs.at[pl.ds(0, 15)], sems.at[1, 0]))
        took(zs.at[pl.ds(0, 15)], sems.at[1, 1])
        pf[step, c, me] = finish(jnp.sum(zs[...], axis=0))
        mine = pf.at[step, c, me]
        for core in (1, 0):
            for dx, dy in PLANE:
                if (dx, dy, core) != (0, 0, 0):
                    device = place((x + dx) % NX, z, (y + dy) % NY, (c + core) % 2)
                    send(mine, mine, (sems.at[2 + core, 0], sems.at[2 + core, 1]), device)
        sent.append((pf.at[step, c, pl.ds(0, 15)], sems.at[2, 0]))
        sent.append((pf.at[step, c], sems.at[3, 0]))
        took(pf.at[step, c, pl.ds(0, 15)], sems.at[2, 1])

    def half_of(step, h):
        return jnp.concatenate([pf[step, h, s] for s in range(16)], axis=0)

    def eliminate(first, last):
        lane = lax.broadcasted_iota(jnp.int32, (RANK, 2 * RANK), 1)
        sub = lax.broadcasted_iota(jnp.int32, (RANK, 1), 0)

        def one(j, carry):
            rows = elim[...]
            pivot = elim[pl.ds(j, 1), :]
            here = lane == (j + RANK)
            column = jnp.sum(jnp.where(here, rows, 0.0), axis=1, keepdims=True)
            diagonal = jnp.sum(jnp.where(here[:1], pivot, 0.0), axis=1, keepdims=True)
            factor = jnp.where(sub > j, column / diagonal, 0.0)
            elim[...] = rows - factor * pivot
            return carry

        lax.fori_loop(first, last, one, 0)

    def inverse():
        lane = lax.broadcasted_iota(jnp.int32, (RANK, 2 * RANK), 1)
        sub = lax.broadcasted_iota(jnp.int32, (RANK, 2 * RANK), 0)
        rows = elim[...]
        diagonal = jnp.sum(jnp.where(lane == sub + RANK, rows, 0.0), axis=1, keepdims=True)
        return rows[:, :RANK] / jnp.sqrt(diagonal)

    def right_sum(step, weight, use):
        sems = q_sem.at[step]
        took(pf.at[step, 1 - c], p_sem.at[step, 3, 1])
        p_sum = jnp.concatenate([half_of(step, 0), half_of(step, 1)], axis=1)
        plain, weighted = tall(p_sum), tall(weight * p_sum)
        for dx in RING4:
            px = (x + dx) % NX
            cols = band_cols(px)
            terms = dot(weighted, g[:, cols], NN) + dot(plain, r[:, cols], NN)
            qs[step, px] = fold(terms).reshape(4, 16, BAND)
            for o in RING4:
                if (dx, o) != (0, 0):
                    pz = window_z(o)
                    send(qs.at[step, px, pz % 4], near.at[step, dx * 4 + o - 1], pair(sems, 0), place(px, pz, y, c))
        sent.append((near.at[step], sems.at[0, 0]))
        diagonal = (
            lax.broadcasted_iota(jnp.int32, (RANK, 2 * RANK), 0)
            == lax.broadcasted_iota(jnp.int32, (RANK, 2 * RANK), 1)
        )
        elim[...] = lax.dot_general(
            p_sum, jnp.concatenate([jnp.zeros_like(p_sum), p_sum], axis=0), NT,
            precision=HIGHEST, preferred_element_type=F32,
        ) + jnp.where(diagonal, 1.0, 0.0)
        eliminate(0, 28)
        took(near.at[step], sems.at[0, 1])
        block = z // 4
        far[step, block] = qs[step, x, z % 4] + jnp.sum(near[step], axis=0)
        for k in (8, 4, 12):
            send(far.at[step, block], far.at[step, block], pair(sems, 1), at_z(k))
        sent.append((far.at[step, pl.ds(0, 3)], sems.at[1, 0]))
        eliminate(28, 64)
        took(far.at[step, pl.ds(0, 3)], sems.at[1, 1])
        qf[step, x, z % 4] = jnp.sum(far[step], axis=0)
        mine = qf.at[step, x, z % 4]
        for dx in RING4:
            for o in RING4:
                if (dx, o) != (0, 0):
                    send(mine, mine, (sems.at[2, 0], spread_sem.at[step, x]), place((x + dx) % NX, window_back(o), y, c))
        for n in range(3):
            sent.append((qf.at[step, n], sems.at[2, 0]))
        sent.append((qf.at[step, 0, pl.ds(0, 3)], sems.at[2, 0]))
        use(inverse(), p_sum)

    def bands(step, inverse_left):
        for dx in (0, 1, 3, 2):
            px = (x + dx) % NX
            if dx == 0:
                took(qf.at[step, x, pl.ds(0, 3)], spread_sem.at[step, x])
            else:
                took(qf.at[step, px], spread_sem.at[step, px])
            band = qf[step, px].reshape(RANK, BAND) * (1.0 / REPLICAS)
            yield dx, band_cols(px), dot(inverse_left, right_factor(band), NN)

    tokens = counts[0].astype(F32)
    load_q.wait()
    first = tall(q0[...])
    load_g.wait()
    load_r.wait()
    for h in (0, 1):
        rows = slice(HALF * h, HALF * (h + 1))
        put_part(part1, h, fold(dot(first, g[rows], NT)) * tokens, 0)
        put_part(part1, h, fold(dot(first, r[rows], NT)), 4)
    count_x[0] = jnp.full((1, 128), tokens, F32)
    pl.semaphore_wait(barrier, PARTNERS)
    for k in (4, 12):
        pl.semaphore_signal(relay, inc=1, device_id=at_z(k), device_id_type=MESH)

    for k in (2, 1, 3):
        send(count_x.at[0], count_x.at[k], pair(count_sem, 0), place((x + k) % NX, z, y, c))
    sent.append((count_x.at[pl.ds(1, 3)], count_sem.at[0, 0]))

    def count_to_z():
        took(count_x.at[pl.ds(1, 3)], count_sem.at[0, 1])
        pl.semaphore_wait(relay, 2)
        count_z[z] = jnp.sum(count_x[...], axis=0)
        for k in RING16:
            send(count_z.at[z], count_z.at[z], pair(count_sem, 1), at_z(k))
        sent.append((count_z.at[pl.ds(0, 15)], count_sem.at[1, 0]))

    def finish_first(total):
        took(count_z.at[pl.ds(0, 15)], count_sem.at[1, 1])
        all_tokens = jnp.sum(count_z[...], axis=0)[:, :1]
        return (total[:4] * (REPLICAS / all_tokens) + total[4:]) * (1.0 / REPLICAS)

    nothing = lambda: None
    left_sum(0, part1, rows1, zs1, nothing, finish_first, count_to_z)
    weight = REPLICAS * tokens / jnp.sum(count_z[...], axis=0)[:, :1]

    kept = []
    right_sum(0, weight, lambda lower_inverse, p_sum: kept.append(left_factor(lower_inverse)))
    inverse_left = kept.pop()

    def left_terms(plain, weighted, rows, cols):
        return fold(dot(weighted, g[rows, cols], NT) + dot(plain, r[rows, cols], NT))

    for dx, cols, band in bands(0, inverse_left):
        plain, weighted = tall(band), tall(weight * band)
        if dx == 0:
            p_acc[...] = left_terms(plain, weighted, slice(None), cols)
        elif dx != 2:
            p_acc[...] = p_acc[...] + left_terms(plain, weighted, slice(None), cols)
    last = cols

    def put_half(h):
        terms = left_terms(plain, weighted, half_rows(h), last)
        put_part(part2, h, p_acc[:, half_rows(h)] + terms, 0)

    put_half(1 - c)

    def own_half():
        put_half(c)

    left_sum(1, part2, rows2, zs2, own_half, lambda total: total * (1.0 / REPLICAS), nothing)

    def last_left(lower_inverse, p_sum):
        p_basis = lax.dot_general(lower_inverse, p_sum, NN, precision=HIGHEST, preferred_element_type=F32)
        high = p_basis.astype(BF16).astype(F32)
        low = p_basis - high
        kept.append(left_factor(lower_inverse))
        kept.append(jnp.concatenate([high, high, low, low], axis=0).T.astype(BF16))
        while len(sent) > 4:
            took(*sent.pop(0))

    right_sum(1, weight, last_left)
    p_left = kept.pop()
    inverse_left = kept.pop()
    for dx, cols, band in bands(1, inverse_left):
        q_final[:, cols] = band
        approx = dot(p_left, right_factor(band), NN)
        matrix = weight * g[:, cols].astype(F32) + r[:, cols].astype(F32)
        new_residual[0, :, cols] = (matrix - approx).astype(BF16)
    for ref, sem in sent:
        took(ref, sem)


def store(residual_in, q_in, residual_out, q_out, sems):
    copies = [
        pltpu.make_async_copy(residual_in, residual_out, sems.at[0]),
        pltpu.make_async_copy(q_in, q_out, sems.at[1]),
    ]
    for copy in copies:
        copy.start()
    for copy in copies:
        copy.wait()


def local(grad, residual, counts, q_start):
    vmem = pl.BlockSpec(memory_space=pltpu.VMEM)
    hbm = pl.BlockSpec(memory_space=pltpu.HBM)
    dma = pltpu.SemaphoreType.DMA
    operands = [pltpu.with_memory_space_constraint(a, pltpu.HBM) for a in (q_start, grad, residual)]
    results = pl.pallas_call(
        kernel,
        out_shape=(
            jax.ShapeDtypeStruct((1, ROWS, WIDTH), BF16),
            jax.ShapeDtypeStruct((RANK, WIDTH), F32),
        ),
        in_specs=[pl.BlockSpec(memory_space=pltpu.SMEM), hbm, hbm, hbm],
        out_specs=(vmem, vmem),
        scratch_shapes=[
            pltpu.VMEM((RANK, WIDTH), F32),
            pltpu.VMEM((ROWS, WIDTH), BF16),
            pltpu.VMEM((ROWS, WIDTH), BF16),
            dma((3,)),
            pltpu.VMEM((4, 1, 128), F32),
            pltpu.VMEM((16, 1, 128), F32),
            dma((2, 2)),
            pltpu.VMEM((2, 16, 8, HALF), F32),
            pltpu.VMEM((31, 8, HALF), F32),
            pltpu.VMEM((16, 8, HALF), F32),
            pltpu.VMEM((2, 16, 4, HALF), F32),
            pltpu.VMEM((31, 4, HALF), F32),
            pltpu.VMEM((16, 4, HALF), F32),
            pltpu.VMEM((2, 2, 16, 4, HALF), F32),
            dma((2, 4, 2)),
            pltpu.VMEM((2, 4, 4, 16, BAND), F32),
            pltpu.VMEM((2, 15, 16, BAND), F32),
            pltpu.VMEM((2, 4, 16, BAND), F32),
            pltpu.VMEM((2, 4, 4, 16, BAND), F32),
            dma((2, 3, 2)),
            dma((2, 4)),
            pltpu.VMEM((RANK, 2 * RANK), F32),
            pltpu.VMEM((RANK, ROWS), F32),
            pltpu.SemaphoreType.REGULAR,
        ],
        compiler_params=pltpu.CompilerParams(
            collective_id=0, has_side_effects=True, vmem_limit_bytes=32 * 1024 * 1024
        ),
        name="power_step",
    )(counts, *operands)
    return pl.pallas_call(
        store,
        out_shape=(
            jax.ShapeDtypeStruct((1, ROWS, WIDTH), BF16),
            jax.ShapeDtypeStruct((RANK, WIDTH), F32),
        ),
        in_specs=[vmem, vmem],
        out_specs=(hbm, hbm),
        scratch_shapes=[dma((2,))],
        name="store",
    )(*(pltpu.with_memory_space_constraint(a, pltpu.VMEM) for a in results))


def solution(mesh):
    placed = (P("dp", None, "tensor"), P("dp", None, "tensor"), P("dp"), P(None, "tensor"))
    return jax.shard_map(
        local,
        mesh=mesh,
        in_specs=placed,
        out_specs=(P("dp", None, "tensor"), P(None, "tensor")),
        check_vma=False,
    )
```
